512 devices in a mesh: grp: 16 (over x, z_lo), mem: 32 (over z_hi, y, core).
Axes of the slice: x: 4, y: 8, z: 8 (z_hi: 2, z_lo: 4; z = z_hi * 4 + z_lo), core: 2. Of those that a mesh axis runs over, the one named last changes fastest.
Arguments:
- points: float32 [16, 262144], P(None, ('grp', 'mem')), may hold values from -6 to 6
- lengthscales: float32 [16], replicated, may hold values from 3 to 12
- probes: float32 [8, 262144], P(None, ('grp', 'mem')), may hold values from -0.25 to 0.25
- plan: int32 [16, 16], replicated, may hold values from 0 to 15, as said below
- round_index: int32 [1], replicated, may hold values from 0 to 15
Outputs:
- product: float32 [8, 262144], P(None, ('grp', 'mem'))
The draws below stay inside these ranges and needn't reach their ends.
Inputs may be any that keep to these rules, and one draw needn't show every extreme that they name: plan[r, g] = g XOR t_r for one t_r of 1 to 15 in each round r, the same for all g, so that each round's pairing is a perfect matching without fixed points.
All inputs are finite; a program needn't handle non-finite values.
Results may differ from the reference program's by a relative error of at most 0.0003.
Values sent between devices are 32-bit elements; how exact they have to be, the bound alone decides.
A program may use at most 64 MiB of HBM per device.

```python
import math
import jax
import jax.numpy as jnp
from jax import lax

FEAT = 16
PROBES = 8
ROUNDS = 16
PTS_DEV = 512
BLOCK = 16384
GROUPS = 16
POINTS = 262144
N_MEM = 32


def draw_plan(key, part):
    key = jax.random.fold_in(key, 1913)
    offsets = jax.random.randint(key, (ROUNDS, 1), 1, GROUPS, dtype=jnp.int32)
    return jnp.bitwise_xor(jnp.arange(GROUPS, dtype=jnp.int32)[None, :], offsets)


def block_scale(stream_key, extent, pieces, least, largest):
    loudness, own = 1.0, jax.random.fold_in(stream_key, 6)
    for axis_at, parts in pieces:
        steps = jnp.exp(jax.random.uniform(jax.random.fold_in(own, axis_at), (parts,), jnp.float32, least / len(pieces), largest / len(pieces)))
        loudness = loudness * jnp.repeat(steps, extent[axis_at] // parts).reshape([-1 if axis == axis_at else 1 for axis in range(len(extent))])
    return loudness


def bell_draw(own_key, dims, spread, limit, cuts=(), kind=jnp.bfloat16):
    entries = jax.random.normal(own_key, dims, jnp.float32) * spread
    if len(cuts) > 0:
        entries = block_scale(own_key, dims, cuts, -0.22, 0.18) * entries
    return jnp.clip(entries, min=-limit, max=limit).astype(kind)


def setup_inputs(seed: int = 0) -> dict:
    streams_of = jax.random.split(jax.random.key(seed), 6)
    return {
        "points": bell_draw(streams_of[0], (FEAT, POINTS), 1.0, 6.0, ((1, 512),), jnp.float32),
        "lengthscales": jnp.clip(jnp.exp(jax.random.uniform(streams_of[1], (FEAT,), jnp.float32, math.log(3.0), math.log(12.0))), 3.0, 12.0),
        "probes": bell_draw(streams_of[2], (PROBES, POINTS), (2.0 * (PTS_DEV * N_MEM) ** -0.5), 0.25, ((1, 512),), jnp.float32),
        "plan": draw_plan(jax.random.fold_in(streams_of[5], 71), 0),
        "round_index": jax.random.randint(streams_of[4], (1,), 0, ROUNDS).astype(jnp.int32),
    }


ROOT_FIVE = math.sqrt(5.0)

def matern(left, right):
    cross = lax.dot_general(left, right, (((0,), (0,)), ((), ())), precision=lax.Precision.HIGHEST, preferred_element_type=jnp.float32)
    dist_sq = lax.optimization_barrier(jnp.sum(left * left, axis=0))[:, None] + lax.optimization_barrier(jnp.sum(right * right, axis=0))[None, :] - 2.0 * cross
    scaled_dist = ROOT_FIVE * jnp.sqrt(jnp.maximum(dist_sq, 0.0))
    return (1.0 + scaled_dist + scaled_dist * scaled_dist / 3.0) * jnp.exp(-scaled_dist)

def reference(points, lengthscales, probes, plan, round_index):
    scaled = points / lengthscales[:, None]
    pairing = plan[round_index[0]]

    def one_row(index):
        group = index // N_MEM
        partner = pairing[group].astype(jnp.int32)
        own = lax.dynamic_slice_in_dim(scaled, (index * PTS_DEV).astype(jnp.int32), PTS_DEV, 1)
        far_pts = lax.dynamic_slice_in_dim(scaled, (partner * BLOCK).astype(jnp.int32), BLOCK, 1)
        far_prb = lax.dynamic_slice_in_dim(probes, (partner * BLOCK).astype(jnp.int32), BLOCK, 1)
        kern = matern(own, far_pts)
        return lax.dot_general(far_prb, kern, (((1,), (1,)), ((), ())), precision=lax.Precision.HIGHEST, preferred_element_type=jnp.float32)
    rows = lax.map(one_row, jnp.arange(GROUPS * N_MEM, dtype=jnp.int32))
    return jnp.transpose(rows, (1, 0, 2)).reshape(PROBES, POINTS)
```

```python
import functools
import math

import jax
import jax.numpy as jnp
from jax import lax
from jax.experimental import pallas as pl
from jax.experimental.pallas import tpu as pltpu
from jax.sharding import PartitionSpec as P

F32, BF16 = jnp.float32, jnp.bfloat16
MESH = pl.DeviceIdType.MESH
LOG2E = math.log2(math.e)
UNIT = math.sqrt(LOG2E / 3.0)
SCALE = math.sqrt(5.0) * UNIT
SLOPE = -LOG2E / UNIT
SHIFT = 3.0 * UNIT * UNIT

FEAT, PROBES, PTS = 16, 8, 512
ROWS = FEAT + PROBES
DEPTH = 128
RING, CORES, HALVES = 8, 2, 2
BLOCKS = RING * CORES * HALVES


def swap_kernel(shift, ls_ref, pts_ref, prb_ref, own_ref, far_ref, send_sem, recv_sem):
    grp, mem = lax.axis_index("grp"), lax.axis_index("mem")
    partner = grp
    for bit in range(4):
        if shift >> bit & 1:
            partner = partner + (1 - 2 * ((grp // (1 << bit)) % 2)) * (1 << bit)
    barrier = pltpu.get_barrier_semaphore()
    pl.semaphore_signal(barrier, inc=1, device_id=(partner, mem), device_id_type=MESH)
    row = lax.broadcasted_iota(jnp.int32, (FEAT, PTS), 0)
    scales = jnp.full((FEAT, PTS), ls_ref[0], F32)
    for feature in range(1, FEAT):
        scales = jnp.where(row == feature, ls_ref[feature], scales)
    own_ref[0:FEAT, :] = pts_ref[...] / scales * SCALE
    own_ref[FEAT:ROWS, :] = prb_ref[...]
    pl.semaphore_wait(barrier, 1)
    copy = pltpu.make_async_remote_copy(
        src_ref=own_ref,
        dst_ref=far_ref,
        send_sem=send_sem,
        recv_sem=recv_sem,
        device_id=(partner, mem),
        device_id_type=MESH,
    )
    copy.start()
    copy.wait()


def swap(shift, ls, points, probes):
    vmem = pl.BlockSpec(memory_space=pltpu.VMEM)
    return pl.pallas_call(
        functools.partial(swap_kernel, shift),
        out_shape=[jax.ShapeDtypeStruct((ROWS, PTS), F32)] * 2,
        in_specs=[pl.BlockSpec(memory_space=pltpu.SMEM), vmem, vmem],
        out_specs=[vmem, vmem],
        scratch_shapes=[pltpu.SemaphoreType.DMA, pltpu.SemaphoreType.DMA],
        compiler_params=pltpu.CompilerParams(collective_id=shift, has_side_effects=True),
        name="swap",
    )(ls, points, probes)


def pieces(x):
    first = x.astype(BF16)
    rest = x - first.astype(F32)
    second = rest.astype(BF16)
    third = (rest - second.astype(F32)).astype(BF16)
    return first, second, third


def lifted(x, left):
    norm = jnp.sum(x * x, axis=0, keepdims=True)
    if left:
        x = x * -2.0
    a, b, c = pieces(x)
    row = lax.broadcasted_iota(jnp.int32, (FEAT, PTS), 0)
    first = 0 if left else 3
    ones = jnp.logical_and(row >= 3 - first, row < 6 - first)
    tail = jnp.where(ones, 1.0, 0.0)
    for index, part in enumerate(pieces(norm)):
        tail = jnp.where(row == first + index, jnp.broadcast_to(part.astype(F32), tail.shape), tail)
    tail = tail.astype(BF16)
    rows = [a, a, b, a, b, c] if left else [a, b, a, c, b, a]
    return jnp.concatenate(rows + [tail, jnp.zeros_like(tail)], 0)


def dot(a, b):
    return lax.dot_general(a, b, (((1,), (0,)), ((), ())), preferred_element_type=F32)


def matern(dist):
    t = jnp.maximum(dist, 1e-30)
    y = t * lax.rsqrt(t) * SLOPE
    return (t - y + SHIFT) * jnp.exp2(y)


UNITS = [
    (0, 0), (-1, 0), (1, 0), (0, 1), (-2, 0), (2, 0), (-1, 1), (1, 1),
    (-3, 0), (3, 0), (-2, 1), (2, 1), (4, 0), (-3, 1), (3, 1), (4, 1),
]
UP_LIMIT = (4, 3)
DOWN_LIMIT = (3, 4)


def block_kernel(
    own_ref, far_ref, out_ref,
    land, left, t0, t1, d0, d1, h0, h1, l0, l1, p0, p1, acc,
    recv_sem, y_sem, sib_sem, z_sem,
):
    grp, mem = lax.axis_index("grp"), lax.axis_index("mem")
    half, ring, core = mem // (RING * CORES), (mem // CORES) % RING, mem % CORES

    def member(h, r, c):
        return (grp, (h * RING + r) * CORES + c)

    up, down = (ring + 1) % RING, (ring + RING - 1) % RING
    to_up, to_down = member(half, up, core), member(half, down, core)
    to_half, to_core = member(1 - half, ring, core), member(half, ring, 1 - core)

    def slot(unit, other_core):
        offset, other_half = UNITS[unit]
        c = 1 - core if other_core else core
        h = 1 - half if other_half else half
        return ((ring + offset + RING) % RING * CORES + c) * HALVES + h

    def copy(where, send_sem, device):
        return pltpu.make_async_remote_copy(
            src_ref=land.at[where],
            dst_ref=land.at[where],
            send_sem=send_sem,
            recv_sem=recv_sem.at[where],
            device_id=device,
            device_id_type=MESH,
        )

    def sends(unit):
        offset, other = UNITS[unit]
        where = slot(unit, False)
        out = [copy(where, sib_sem.at[unit], to_core)]
        if unit == 0:
            out.append(copy(where, z_sem, to_half))
        if -UP_LIMIT[other] < offset <= 0:
            out.append(copy(where, y_sem.at[unit, 0], to_up))
        if 0 <= offset < DOWN_LIMIT[other] and not (offset == 4):
            out.append(copy(where, y_sem.at[unit, 1], to_down))
        return out

    def arrived(where):
        copy(where, z_sem, to_half).wait_recv()

    barrier = pltpu.get_barrier_semaphore()
    for device in (to_up, to_down, to_half, to_core):
        pl.semaphore_signal(barrier, inc=1, device_id=device, device_id_type=MESH)
    land[slot(0, False)] = far_ref[...]
    left[...] = lifted(own_ref[0:FEAT, :], True)
    acc[...] = jnp.zeros_like(acc)
    h1[...] = jnp.zeros_like(h1)
    l1[...] = jnp.zeros_like(l1)
    p1[...] = jnp.zeros_like(p1)
    T, D, H, L, W = (t0, t1), (d0, d1), (h0, h1), (l0, l1), (p0, p1)

    def lift(where, k):
        T[k][...] = lifted(land[where, 0:FEAT, :], False).T

    def distances(k):
        D[k][...] = dot(T[k][...], left[...])

    def step(where, ahead, k):
        o = 1 - k
        for r in range(0, PTS, 256):
            for c in range(0, PTS, 256):
                rows, cols = slice(r, r + 256), slice(c, c + 256)
                value = matern(D[k][rows, cols])
                high = value.astype(BF16)
                H[k][rows, cols] = high
                L[k][rows, cols] = (value - high.astype(F32)).astype(BF16)
                D[o][rows, cols] = dot(T[o][rows, :], left[:, cols])
                weights = W[o][:, rows]
                acc[:, cols] += dot(weights, H[o][rows, cols]) + dot(weights, L[o][rows, cols])
        probes = land[where, FEAT:ROWS, :]
        high = probes.astype(BF16)
        W[k][...] = jnp.concatenate([high, (probes - high.astype(F32)).astype(BF16)], 0)
        lift(ahead, k)

    pl.semaphore_wait(barrier, 4)
    for item in sends(0):
        item.start()
    lift(slot(0, False), 0)
    distances(0)
    arrived(slot(0, True))
    lift(slot(0, True), 1)

    def picked(index, values):
        result = values[0]
        for at in range(1, len(values)):
            result = jnp.where(index == at, values[at], result)
        return result

    n_units = len(UNITS)
    slots = [slot(unit, other) for unit in range(n_units) for other in (False, True)]
    slots += [slots[-2], slots[-1]]

    def body(n, carry):
        for m in range(n_units // 2):
            @pl.when(n == m)
            def _():
                for unit in (2 * m + 1, 2 * m + 2):
                    if unit < n_units:
                        arrived(slot(unit, False))
                        for item in sends(unit):
                            item.start()
                for unit in (2 * m + 1, 2 * m + 2):
                    if unit < n_units:
                        arrived(slot(unit, True))
        here = [picked(n, slots[at::4][:n_units // 2]) for at in range(4)]
        ahead = here[2:] + [picked(n, slots[at + 4::4][:n_units // 2]) for at in range(2)]
        for q in range(4):
            step(here[q], ahead[q], q % 2)
        return carry

    lax.fori_loop(0, n_units // 2, body, 0)
    acc[...] += dot(p1[...], h1[...]) + dot(p1[...], l1[...])
    out_ref[...] = (acc[0:PROBES, :] + acc[PROBES : 2 * PROBES, :]) * (1.0 / SHIFT)
    for unit in range(n_units):
        for item in sends(unit):
            item.wait_send()


def blocks(own, far):
    vmem = pl.BlockSpec(memory_space=pltpu.VMEM)
    return pl.pallas_call(
        block_kernel,
        out_shape=jax.ShapeDtypeStruct((PROBES, PTS), F32),
        in_specs=[vmem, vmem],
        out_specs=vmem,
        scratch_shapes=[
            pltpu.VMEM((BLOCKS, ROWS, PTS), F32),
            pltpu.VMEM((DEPTH, PTS), BF16),
            pltpu.VMEM((PTS, DEPTH), BF16),
            pltpu.VMEM((PTS, DEPTH), BF16),
            pltpu.VMEM((PTS, PTS), F32),
            pltpu.VMEM((PTS, PTS), F32),
            pltpu.VMEM((PTS, PTS), BF16),
            pltpu.VMEM((PTS, PTS), BF16),
            pltpu.VMEM((PTS, PTS), BF16),
            pltpu.VMEM((PTS, PTS), BF16),
            pltpu.VMEM((2 * PROBES, PTS), BF16),
            pltpu.VMEM((2 * PROBES, PTS), BF16),
            pltpu.VMEM((2 * PROBES, PTS), F32),
            pltpu.SemaphoreType.DMA((BLOCKS,)),
            pltpu.SemaphoreType.DMA((len(UNITS), 2)),
            pltpu.SemaphoreType.DMA((len(UNITS),)),
            pltpu.SemaphoreType.DMA,
        ],
        compiler_params=pltpu.CompilerParams(
            collective_id=0, has_side_effects=True, vmem_limit_bytes=32 << 20
        ),
        name="blocks",
    )(own, far)


def shards(points, lengthscales, probes, plan, round_index):
    shift = plan[round_index[0], 0]
    own, far = lax.switch(
        shift - 1,
        [functools.partial(swap, which) for which in range(1, 16)],
        lengthscales, points, probes,
    )
    return blocks(own, far)


def solution(mesh):
    in_specs = (P(None, ("grp", "mem")), P(), P(None, ("grp", "mem")), P(), P())
    out_specs = P(None, ("grp", "mem"))
    return jax.shard_map(shards, mesh=mesh, in_specs=in_specs, out_specs=out_specs, check_vma=False)
```

```python
import functools
import math

import jax
import jax.numpy as jnp
from jax import lax
from jax.experimental import pallas as pl
from jax.experimental.pallas import tpu as pltpu
from jax.sharding import PartitionSpec as P

F32, BF16 = jnp.float32, jnp.bfloat16
MESH = pl.DeviceIdType.MESH
LOG2E = math.log2(math.e)
UNIT = math.sqrt(LOG2E / 3.0)
SCALE = math.sqrt(5.0) * UNIT
SLOPE = -LOG2E / UNIT
SHIFT = 3.0 * UNIT * UNIT

FEAT, PROBES, PTS = 16, 8, 512
ROWS = FEAT + PROBES
DEPTH = 128
RING, CORES, HALVES = 8, 2, 2


def pieces(x):
    first = x.astype(BF16)
    rest = x - first.astype(F32)
    second = rest.astype(BF16)
    third = (rest - second.astype(F32)).astype(BF16)
    return first, second, third


def lifted(x, left):
    norm = jnp.sum(x * x, axis=0, keepdims=True)
    if left:
        x = x * -2.0
    a, b, c = pieces(x)
    row = lax.broadcasted_iota(jnp.int32, (FEAT, PTS), 0)
    first = 0 if left else 3
    ones = jnp.logical_and(row >= 3 - first, row < 6 - first)
    tail = jnp.where(ones, 1.0, 0.0)
    for index, part in enumerate(pieces(norm)):
        tail = jnp.where(row == first + index, jnp.broadcast_to(part.astype(F32), tail.shape), tail)
    tail = tail.astype(BF16)
    rows = [a, a, b, a, b, c] if left else [a, b, a, c, b, a]
    return jnp.concatenate(rows + [tail, jnp.zeros_like(tail)], 0)


def dot(a, b):
    return lax.dot_general(a, b, (((1,), (0,)), ((), ())), preferred_element_type=F32)


def matern(dist):
    t = jnp.maximum(dist, 1e-30)
    y = t * lax.rsqrt(t) * SLOPE
    return (t - y + SHIFT) * jnp.exp2(y)


OWN, CORE, HALF, BOTH = range(4)
STEPS = (0, 1, -1, 2, -2, 3, -3, 4)
PAIRS = [(OWN, 0), (CORE, 0), (HALF, 0), (BOTH, 0)]
PAIRS += [(who, block) for block in range(1, RING) for who in (HALF, BOTH)]
PAIRS += [(CORE, block) for block in range(1, RING)]
PAIRS += [(OWN, block) for block in range(1, RING)]
GROUP = 4
GROUPS = len(PAIRS) // GROUP


def block_kernel(
    shift, ls_ref, pts_ref, prb_ref, out_ref,
    stage, there, land, left, right, probes, d0, d1, h0, h1, l0, l1, acc, part, back,
    land_sem, there_sem, back_sem, swap_sem, ring_sem, near_sem, part_sem,
):
    grp, mem = lax.axis_index("grp"), lax.axis_index("mem")
    half, ring, core = mem // (RING * CORES), (mem // CORES) % RING, mem % CORES
    partner = grp
    for bit in range(4):
        if shift >> bit & 1:
            partner = partner + (1 - 2 * ((grp // (1 << bit)) % 2)) * (1 << bit)

    def member(h, r, c):
        return (grp, (h * RING + r) * CORES + c)

    def place(step):
        return (ring + step + RING) % RING

    across = (partner, mem)
    around = [member(half, place(step), core) for step in STEPS]
    near = [None, member(half, ring, 1 - core), member(1 - half, ring, core), member(1 - half, ring, 1 - core)]

    barrier = pltpu.get_barrier_semaphore()
    for device in [across] + around[1:] + near[1:]:
        pl.semaphore_signal(barrier, inc=1, device_id=device, device_id_type=MESH)

    def remote(src, dst, send_sem, recv_sem, device):
        return pltpu.make_async_remote_copy(
            src_ref=src, dst_ref=dst, send_sem=send_sem, recv_sem=recv_sem,
            device_id=device, device_id_type=MESH,
        )

    swap = remote(stage, land.at[ring], swap_sem, land_sem.at[ring], across)
    points_to = [
        remote(stage.at[0:FEAT], there.at[who - 1], near_sem.at[who - 1], there_sem.at[who - 1], near[who])
        for who in (CORE, HALF, BOTH)
    ]
    ring_to = [
        remote(land.at[ring], land.at[ring], ring_sem.at[at - 1], land_sem.at[ring], around[at])
        for at in range(1, RING)
    ]
    sums_to = [
        remote(part.at[who - 1], back.at[who - 1], part_sem.at[who - 1], back_sem.at[who - 1], near[who])
        for who in (CORE, HALF, BOTH)
    ]

    def block_arrived(at):
        where = place(STEPS[at])
        remote(land.at[where], land.at[where], swap_sem, land_sem.at[where], across).wait_recv()

    D, H, L = (d0, d1), (h0, h1), (l0, l1)

    def lift(at):
        where = place(STEPS[at])
        right[where] = lifted(land[where, 0:FEAT, :], False).T
        values = land[where, FEAT:ROWS, :]
        high = values.astype(BF16)
        probes[where] = jnp.concatenate([high, (values - high.astype(F32)).astype(BF16)], 0)

    def distances(pair, k):
        who, where = pair
        D[k][...] = dot(right[where], left[who])

    def products(pair, k):
        who, where = pair
        acc[who] += dot(probes[where], H[k][...]) + dot(probes[where], L[k][...])

    def step(pair, ahead, behind, k):
        o = 1 - k
        for r in range(0, PTS, 256):
            for c in range(0, PTS, 256):
                rows, cols = slice(r, r + 256), slice(c, c + 256)
                value = matern(D[k][rows, cols])
                high = value.astype(BF16)
                H[k][rows, cols] = high
                L[k][rows, cols] = (value - high.astype(F32)).astype(BF16)
                if ahead is not None:
                    D[o][rows, cols] = dot(right[ahead[1], rows, :], left[ahead[0], :, cols])
                if behind is not None:
                    weights = probes[behind[1], :, rows]
                    acc[behind[0], :, cols] += dot(weights, H[o][rows, cols]) + dot(weights, L[o][rows, cols])

    row = lax.broadcasted_iota(jnp.int32, (FEAT, PTS), 0)
    scales = jnp.full((FEAT, PTS), ls_ref[0], F32)
    for feature in range(1, FEAT):
        scales = jnp.where(row == feature, ls_ref[feature], scales)
    stage[0:FEAT, :] = pts_ref[...] / scales * SCALE
    stage[FEAT:ROWS, :] = prb_ref[...]
    left[OWN] = lifted(stage[0:FEAT, :], True)
    acc[...] = jnp.zeros_like(acc)

    pl.semaphore_wait(barrier, 11)
    swap.start()
    for item in points_to:
        item.start()
    points_to[0].wait_recv()
    left[CORE] = lifted(there[CORE - 1], True)
    block_arrived(0)
    for item in ring_to:
        item.start()
    lift(0)
    pairs = [(who, place(STEPS[at])) for who, at in PAIRS]
    distances(pairs[0], 0)
    for who in (HALF, BOTH):
        points_to[who - 1].wait_recv()
        left[who] = lifted(there[who - 1], True)
    for q in range(GROUP):
        step(pairs[q], pairs[q + 1] if q + 1 < GROUP else None, pairs[q - 1] if q else None, q % 2)
    block_arrived(1)
    lift(1)
    distances(pairs[GROUP], 0)

    def picked(index, values):
        result = values[0]
        for at in range(1, len(values)):
            result = jnp.where(index == at, values[at], result)
        return result

    whos = [who for who, _ in PAIRS]
    wheres = [where for _, where in pairs]

    def pair_at(n, q):
        at = [min(g * GROUP + q, len(PAIRS) - 1) for g in range(GROUPS)]
        return picked(n, [whos[i] for i in at]), picked(n, [wheres[i] for i in at])

    def send_sum(who):
        part[who - 1] = acc[who, 0:PROBES, :] + acc[who, PROBES : 2 * PROBES, :]
        sums_to[who - 1].start()

    def body(n, carry):
        for m in (1, 2, 3):
            @pl.when(n == m)
            def _():
                for at in (2 * m, 2 * m + 1):
                    block_arrived(at)
                    lift(at)

        @pl.when(n == 5)
        def _():
            send_sum(HALF)
            send_sum(BOTH)

        @pl.when(n == 7)
        def _():
            send_sum(CORE)

        seq = [pair_at(n, q) for q in range(-1, GROUP + 1)]
        for q in range(GROUP):
            step(seq[q + 1], seq[q + 2], seq[q], q % 2)
        return carry

    lax.fori_loop(1, GROUPS, body, 0)
    products(pairs[-1], 1)
    total = acc[OWN, 0:PROBES, :] + acc[OWN, PROBES : 2 * PROBES, :]
    for who in (HALF, BOTH, CORE):
        sums_to[who - 1].wait_recv()
        total += back[who - 1]
    out_ref[...] = total * (1.0 / SHIFT)
    for item in [swap] + points_to + ring_to + sums_to:
        item.wait_send()


def blocks(shift, ls, points, probes):
    vmem = pl.BlockSpec(memory_space=pltpu.VMEM)
    dma = pltpu.SemaphoreType.DMA
    return pl.pallas_call(
        functools.partial(block_kernel, shift),
        out_shape=jax.ShapeDtypeStruct((PROBES, PTS), F32),
        in_specs=[pl.BlockSpec(memory_space=pltpu.SMEM), vmem, vmem],
        out_specs=vmem,
        scratch_shapes=[
            pltpu.VMEM((ROWS, PTS), F32),
            pltpu.VMEM((3, FEAT, PTS), F32),
            pltpu.VMEM((RING, ROWS, PTS), F32),
            pltpu.VMEM((4, DEPTH, PTS), BF16),
            pltpu.VMEM((RING, PTS, DEPTH), BF16),
            pltpu.VMEM((RING, 2 * PROBES, PTS), BF16),
            pltpu.VMEM((PTS, PTS), F32),
            pltpu.VMEM((PTS, PTS), F32),
            pltpu.VMEM((PTS, PTS), BF16),
            pltpu.VMEM((PTS, PTS), BF16),
            pltpu.VMEM((PTS, PTS), BF16),
            pltpu.VMEM((PTS, PTS), BF16),
            pltpu.VMEM((4, 2 * PROBES, PTS), F32),
            pltpu.VMEM((3, PROBES, PTS), F32),
            pltpu.VMEM((3, PROBES, PTS), F32),
            dma((RING,)), dma((3,)), dma((3,)), dma, dma((RING - 1,)), dma((3,)), dma((3,)),
        ],
        compiler_params=pltpu.CompilerParams(
            collective_id=shift, has_side_effects=True, vmem_limit_bytes=32 << 20
        ),
        name="blocks",
    )(ls, points, probes)


def shards(points, lengthscales, probes, plan, round_index):
    shift = plan[round_index[0], 0]
    return lax.switch(
        shift - 1,
        [functools.partial(blocks, which) for which in range(1, 16)],
        lengthscales, points, probes,
    )


def solution(mesh):
    in_specs = (P(None, ("grp", "mem")), P(), P(None, ("grp", "mem")), P(), P())
    out_specs = P(None, ("grp", "mem"))
    return jax.shard_map(shards, mesh=mesh, in_specs=in_specs, out_specs=out_specs, check_vma=False)
```

```python
import functools
import math

import jax
import jax.numpy as jnp
from jax import lax
from jax.experimental import pallas as pl
from jax.experimental.pallas import tpu as pltpu
from jax.sharding import PartitionSpec as P

F32, BF16 = jnp.float32, jnp.bfloat16
MESH = pl.DeviceIdType.MESH
LOG2E = math.log2(math.e)
UNIT = math.sqrt(LOG2E / 3.0)
SCALE = math.sqrt(5.0) * UNIT
SLOPE = -LOG2E / UNIT
SHIFT = 3.0 * UNIT * UNIT

FEAT, PROBES, PTS = 16, 8, 512
ROWS = FEAT + PROBES
DEPTH = 128
RING, CORES, HALVES = 8, 2, 2


def coordinates():
    grp, mem = lax.axis_index("grp"), lax.axis_index("mem")
    return grp, mem // (RING * CORES), (mem // CORES) % RING, mem % CORES


def member(grp, half, ring, core):
    return (grp, (half * RING + ring) * CORES + core)


def near_devices():
    grp, half, ring, core = coordinates()
    return [
        member(grp, half, ring, 1 - core),
        member(grp, 1 - half, ring, core),
        member(grp, 1 - half, ring, 1 - core),
    ]


def remote(src, dst, send_sem, recv_sem, device):
    return pltpu.make_async_remote_copy(
        src_ref=src, dst_ref=dst, send_sem=send_sem, recv_sem=recv_sem,
        device_id=device, device_id_type=MESH,
    )


def enter(devices):
    barrier = pltpu.get_barrier_semaphore()
    for device in devices:
        pl.semaphore_signal(barrier, inc=1, device_id=device, device_id_type=MESH)
    return barrier


def scale_kernel(round_ref, plan_ref, ls_ref, pts_ref, prb_ref, shift_ref, own_ref):
    shift_ref[0] = plan_ref[round_ref[0], 0] - 1
    row = lax.broadcasted_iota(jnp.int32, (FEAT, PTS), 0)
    scales = jnp.full((FEAT, PTS), ls_ref[0], F32)
    for feature in range(1, FEAT):
        scales = jnp.where(row == feature, ls_ref[feature], scales)
    own_ref[0:FEAT, :] = pts_ref[...] / scales * SCALE
    own_ref[FEAT:ROWS, :] = prb_ref[...]


def scale(round_index, plan, ls, points, probes):
    vmem, smem = pl.BlockSpec(memory_space=pltpu.VMEM), pl.BlockSpec(memory_space=pltpu.SMEM)
    return pl.pallas_call(
        scale_kernel,
        out_shape=[jax.ShapeDtypeStruct((1,), jnp.int32), jax.ShapeDtypeStruct((ROWS, PTS), F32)],
        in_specs=[smem, smem, smem, vmem, vmem],
        out_specs=[smem, vmem],
        name="scale",
    )(round_index, plan, ls, points, probes)


def swap_kernel(shift, own_ref, far_ref, there_ref, send_sem, recv_sem):
    grp, half, ring, core = coordinates()
    partner = grp
    for bit in range(4):
        if shift >> bit & 1:
            partner = partner + (1 - 2 * ((grp // (1 << bit)) % 2)) * (1 << bit)
    devices = [member(partner, half, ring, core), member(grp, half, ring, 1 - core)]
    barrier = enter(devices)
    pl.semaphore_wait(barrier, len(devices))
    copies = [
        remote(own_ref, far_ref, send_sem.at[0], recv_sem.at[0], devices[0]),
        remote(own_ref.at[0:FEAT], there_ref, send_sem.at[1], recv_sem.at[1], devices[1]),
    ]
    for copy in copies:
        copy.start()
    for copy in copies:
        copy.wait()


def swap(shift, own):
    vmem = pl.BlockSpec(memory_space=pltpu.VMEM)
    return pl.pallas_call(
        functools.partial(swap_kernel, shift),
        out_shape=[jax.ShapeDtypeStruct((ROWS, PTS), F32), jax.ShapeDtypeStruct((FEAT, PTS), F32)],
        in_specs=[vmem],
        out_specs=[vmem] * 2,
        scratch_shapes=[pltpu.SemaphoreType.DMA((2,)), pltpu.SemaphoreType.DMA((2,))],
        compiler_params=pltpu.CompilerParams(collective_id=shift, has_side_effects=True),
        name="swap",
    )(own)


def pieces(x):
    first = x.astype(BF16)
    rest = x - first.astype(F32)
    second = rest.astype(BF16)
    third = (rest - second.astype(F32)).astype(BF16)
    return first, second, third


def lifted(x, left):
    norm = jnp.sum(x * x, axis=0, keepdims=True)
    if left:
        x = x * -2.0
    a, b, c = pieces(x)
    row = lax.broadcasted_iota(jnp.int32, (FEAT, PTS), 0)
    first = 0 if left else 3
    ones = jnp.logical_and(row >= 3 - first, row < 6 - first)
    tail = jnp.where(ones, 1.0, 0.0)
    for index, part in enumerate(pieces(norm)):
        tail = jnp.where(row == first + index, jnp.broadcast_to(part.astype(F32), tail.shape), tail)
    tail = tail.astype(BF16)
    rows = [a, a, b, a, b, c] if left else [a, b, a, c, b, a]
    return jnp.concatenate(rows + [tail, jnp.zeros_like(tail)], 0)


def dot(a, b):
    return lax.dot_general(a, b, (((1,), (0,)), ((), ())), preferred_element_type=F32)


def matern(dist):
    t = jnp.maximum(dist, 1e-30)
    y = t * lax.rsqrt(t) * SLOPE
    return (t - y + SHIFT) * jnp.exp2(y)


OWN, CORE, HALF, BOTH = range(4)
STEPS = (0, 1, -1, 2, -2, 3, -3, 4)
PAIRS = [(OWN, 0), (CORE, 0), (OWN, 1), (CORE, 1), (OWN, 2), (CORE, 2), (CORE, 3)]
PAIRS += [(who, block) for first in (0, 4) for who in (HALF, BOTH) for block in range(first, first + 4)]
PAIRS += [(CORE, block) for block in range(4, RING)]
PAIRS += [(OWN, block) for block in range(3, RING)]
GROUP = 4
GROUPS = len(PAIRS) // GROUP
READY = {1: (3,), 3: (4, 5), 4: (6, 7)}


def block_kernel(
    own_ref, far_ref, there_ref, out_ref,
    land, other, left, right, probes, d0, d1, h0, h1, l0, l1, acc, part, back,
    land_sem, back_sem, ring_sem, part_sem, other_send, other_recv,
):
    grp, half, ring, core = coordinates()

    def place(step):
        return (ring + step + RING) % RING

    around = [member(grp, half, place(step), core) for step in STEPS]
    near = near_devices()
    barrier = enter(around[1:] + near)
    ring_to = [
        remote(far_ref, land.at[ring], ring_sem.at[at - 1], land_sem.at[ring], around[at])
        for at in range(1, RING)
    ]
    half_to = remote(own_ref.at[0:FEAT], other.at[0], other_send.at[0], other_recv.at[0], near[1])
    both_to = remote(other.at[0], other.at[1], other_send.at[1], other_recv.at[1], near[0])
    sums_to = [remote(part.at[at], back.at[at], part_sem.at[at], back_sem.at[at], near[at]) for at in range(3)]

    def block_arrived(at):
        where = place(STEPS[at])
        remote(far_ref, land.at[where], ring_sem.at[0], land_sem.at[where], around[at]).wait_recv()

    D, H, L = (d0, d1), (h0, h1), (l0, l1)

    def lift(at):
        where = place(STEPS[at])
        block = land.at[where] if at else far_ref
        right[where] = lifted(block[0:FEAT, :], False).T
        values = block[FEAT:ROWS, :]
        high = values.astype(BF16)
        probes[where] = jnp.concatenate([high, (values - high.astype(F32)).astype(BF16)], 0)

    def distances(pair, k):
        who, where = pair
        D[k][...] = dot(right[where], left[who])

    def products(pair, k):
        who, where = pair
        acc[who] += dot(probes[where], H[k][...]) + dot(probes[where], L[k][...])

    def step(pair, ahead, behind, k):
        o = 1 - k
        for r in range(0, PTS, 256):
            for c in range(0, PTS, 256):
                rows, cols = slice(r, r + 256), slice(c, c + 256)
                value = matern(D[k][rows, cols])
                high = value.astype(BF16)
                H[k][rows, cols] = high
                L[k][rows, cols] = (value - high.astype(F32)).astype(BF16)
                if ahead is not None:
                    D[o][rows, cols] = dot(right[ahead[1], rows, :], left[ahead[0], :, cols])
                if behind is not None:
                    weights = probes[behind[1], :, rows]
                    acc[behind[0], :, cols] += dot(weights, H[o][rows, cols]) + dot(weights, L[o][rows, cols])

    pairs = [(who, place(STEPS[at])) for who, at in PAIRS]
    left[OWN] = lifted(own_ref[0:FEAT, :], True)
    lift(0)
    distances(pairs[0], 0)
    left[CORE] = lifted(there_ref[...], True)
    acc[...] = jnp.zeros_like(acc)
    step(pairs[0], pairs[1], None, 0)
    step(pairs[1], None, pairs[0], 1)
    pl.semaphore_wait(barrier, RING - 1 + 3)
    ring_to[0].start()
    ring_to[1].start()
    half_to.start()
    for item in ring_to[2:]:
        item.start()
    for at in (1, 2):
        block_arrived(at)
        lift(at)
    distances(pairs[2], 0)
    step(pairs[2], pairs[3], pairs[1], 0)
    step(pairs[3], pairs[4], pairs[2], 1)

    def picked(index, values):
        result = values[0]
        for at in range(1, len(values)):
            result = jnp.where(index == at, values[at], result)
        return result

    whos = [who for who, _ in PAIRS]
    wheres = [where for _, where in pairs]

    def pair_at(n, q):
        at = [min(g * GROUP + q, len(PAIRS) - 1) for g in range(GROUPS)]
        return picked(n, [whos[i] for i in at]), picked(n, [wheres[i] for i in at])

    def send_sum(who):
        part[who - 1] = acc[who, 0:PROBES, :] + acc[who, PROBES : 2 * PROBES, :]
        sums_to[who - 1].start()

    def body(n, carry):
        for m, blocks_ready in READY.items():
            @pl.when(n == m)
            def _():
                for at in blocks_ready:
                    block_arrived(at)
                    lift(at)

        @pl.when(n == 1)
        def _():
            half_to.wait_recv()
            both_to.start()
            left[HALF] = lifted(other[0], True)

        @pl.when(n == 2)
        def _():
            both_to.wait_recv()
            left[BOTH] = lifted(other[1], True)

        @pl.when(n == 6)
        def _():
            send_sum(HALF)
            send_sum(BOTH)

        @pl.when(n == 7)
        def _():
            send_sum(CORE)

        seq = [pair_at(n, q) for q in range(-1, GROUP + 1)]
        for q in range(GROUP):
            step(seq[q + 1], seq[q + 2], seq[q], q % 2)
        return carry

    lax.fori_loop(1, GROUPS, body, 0)
    products(pairs[-1], 1)
    total = acc[OWN, 0:PROBES, :] + acc[OWN, PROBES : 2 * PROBES, :]
    for who in (HALF, BOTH, CORE):
        sums_to[who - 1].wait_recv()
        total += back[who - 1]
    out_ref[...] = total * (1.0 / SHIFT)
    for item in ring_to + [half_to, both_to] + sums_to:
        item.wait_send()


def blocks(own, far, there):
    vmem = pl.BlockSpec(memory_space=pltpu.VMEM)
    dma = pltpu.SemaphoreType.DMA
    return pl.pallas_call(
        block_kernel,
        out_shape=jax.ShapeDtypeStruct((PROBES, PTS), F32),
        in_specs=[vmem] * 3,
        out_specs=vmem,
        scratch_shapes=[
            pltpu.VMEM((RING, ROWS, PTS), F32),
            pltpu.VMEM((2, FEAT, PTS), F32),
            pltpu.VMEM((4, DEPTH, PTS), BF16),
            pltpu.VMEM((RING, PTS, DEPTH), BF16),
            pltpu.VMEM((RING, 2 * PROBES, PTS), BF16),
            pltpu.VMEM((PTS, PTS), F32),
            pltpu.VMEM((PTS, PTS), F32),
            pltpu.VMEM((PTS, PTS), BF16),
            pltpu.VMEM((PTS, PTS), BF16),
            pltpu.VMEM((PTS, PTS), BF16),
            pltpu.VMEM((PTS, PTS), BF16),
            pltpu.VMEM((4, 2 * PROBES, PTS), F32),
            pltpu.VMEM((3, PROBES, PTS), F32),
            pltpu.VMEM((3, PROBES, PTS), F32),
            dma((RING,)), dma((3,)), dma((RING - 1,)), dma((3,)), dma((2,)), dma((2,)),
        ],
        compiler_params=pltpu.CompilerParams(
            collective_id=0, has_side_effects=True, vmem_limit_bytes=32 << 20
        ),
        name="blocks",
    )(own, far, there)


def shards(points, lengthscales, probes, plan, round_index):
    shift, own = scale(round_index, plan, lengthscales, points, probes)
    far, there = lax.switch(shift[0], [functools.partial(swap, which) for which in range(1, 16)], own)
    return blocks(own, far, there)


def solution(mesh):
    in_specs = (P(None, ("grp", "mem")), P(), P(None, ("grp", "mem")), P(), P())
    out_specs = P(None, ("grp", "mem"))
    return jax.shard_map(shards, mesh=mesh, in_specs=in_specs, out_specs=out_specs, check_vma=False)
```

```python
import functools
import math

import jax
import jax.numpy as jnp
from jax import lax
from jax.experimental import pallas as pl
from jax.experimental.pallas import tpu as pltpu
from jax.sharding import PartitionSpec as P

F32, BF16 = jnp.float32, jnp.bfloat16
MESH = pl.DeviceIdType.MESH
LOG2E = math.log2(math.e)
UNIT = math.sqrt(LOG2E / 3.0)
SCALE = math.sqrt(5.0) * UNIT
SLOPE = -LOG2E / UNIT
SHIFT = 3.0 * UNIT * UNIT

FEAT, PROBES, PTS = 16, 8, 512
ROWS = FEAT + PROBES
DEPTH = 128
RING, CORES, HALVES = 8, 2, 2


def coordinates():
    grp, mem = lax.axis_index("grp"), lax.axis_index("mem")
    return grp, mem // (RING * CORES), (mem // CORES) % RING, mem % CORES


def member(grp, half, ring, core):
    return (grp, (half * RING + ring) * CORES + core)


def near_devices():
    grp, half, ring, core = coordinates()
    return [
        member(grp, half, ring, 1 - core),
        member(grp, 1 - half, ring, core),
        member(grp, 1 - half, ring, 1 - core),
    ]


def remote(src, dst, send_sem, recv_sem, device):
    return pltpu.make_async_remote_copy(
        src_ref=src, dst_ref=dst, send_sem=send_sem, recv_sem=recv_sem,
        device_id=device, device_id_type=MESH,
    )


def enter(devices):
    barrier = pltpu.get_barrier_semaphore()
    for device in devices:
        pl.semaphore_signal(barrier, inc=1, device_id=device, device_id_type=MESH)
    return barrier


def scale_kernel(round_ref, plan_ref, ls_ref, pts_ref, prb_ref, shift_ref, own_ref):
    shift_ref[0] = plan_ref[round_ref[0], 0] - 1
    row = lax.broadcasted_iota(jnp.int32, (FEAT, PTS), 0)
    scales = jnp.full((FEAT, PTS), ls_ref[0], F32)
    for feature in range(1, FEAT):
        scales = jnp.where(row == feature, ls_ref[feature], scales)
    own_ref[0:FEAT, :] = pts_ref[...] / scales * SCALE
    own_ref[FEAT:ROWS, :] = prb_ref[...]


def scale(round_index, plan, ls, points, probes):
    vmem, smem = pl.BlockSpec(memory_space=pltpu.VMEM), pl.BlockSpec(memory_space=pltpu.SMEM)
    return pl.pallas_call(
        scale_kernel,
        out_shape=[jax.ShapeDtypeStruct((1,), jnp.int32), jax.ShapeDtypeStruct((ROWS, PTS), F32)],
        in_specs=[smem, smem, smem, vmem, vmem],
        out_specs=[smem, vmem],
        name="scale",
    )(round_index, plan, ls, points, probes)


def swap_kernel(shift, own_ref, far_ref, there_ref, send_sem, recv_sem):
    grp, half, ring, core = coordinates()
    partner = grp
    for bit in range(4):
        if shift >> bit & 1:
            partner = partner + (1 - 2 * ((grp // (1 << bit)) % 2)) * (1 << bit)
    devices = [member(partner, half, ring, core), member(grp, half, ring, 1 - core)]
    barrier = enter(devices)
    pl.semaphore_wait(barrier, len(devices))
    copies = [
        remote(own_ref, far_ref, send_sem.at[0], recv_sem.at[0], devices[0]),
        remote(own_ref.at[0:FEAT], there_ref, send_sem.at[1], recv_sem.at[1], devices[1]),
    ]
    for copy in copies:
        copy.start()
    for copy in copies:
        copy.wait()


def swap(shift, own):
    vmem = pl.BlockSpec(memory_space=pltpu.VMEM)
    return pl.pallas_call(
        functools.partial(swap_kernel, shift),
        out_shape=[jax.ShapeDtypeStruct((ROWS, PTS), F32), jax.ShapeDtypeStruct((FEAT, PTS), F32)],
        in_specs=[vmem],
        out_specs=[vmem] * 2,
        scratch_shapes=[pltpu.SemaphoreType.DMA((2,)), pltpu.SemaphoreType.DMA((2,))],
        compiler_params=pltpu.CompilerParams(collective_id=shift, has_side_effects=True),
        name="swap",
    )(own)


def pieces(x):
    first = x.astype(BF16)
    rest = x - first.astype(F32)
    second = rest.astype(BF16)
    third = (rest - second.astype(F32)).astype(BF16)
    return first, second, third


def lifted(x, left):
    norm = jnp.sum(x * x, axis=0, keepdims=True)
    if left:
        x = x * -2.0
    a, b, c = pieces(x)
    row = lax.broadcasted_iota(jnp.int32, (FEAT, PTS), 0)
    first = 0 if left else 3
    ones = jnp.logical_and(row >= 3 - first, row < 6 - first)
    tail = jnp.where(ones, 1.0, 0.0)
    for index, part in enumerate(pieces(norm)):
        tail = jnp.where(row == first + index, jnp.broadcast_to(part.astype(F32), tail.shape), tail)
    tail = tail.astype(BF16)
    rows = [a, a, b, a, b, c] if left else [a, b, a, c, b, a]
    return jnp.concatenate(rows + [tail, jnp.zeros_like(tail)], 0)


def dot(a, b):
    return lax.dot_general(a, b, (((1,), (0,)), ((), ())), preferred_element_type=F32)


def matern(dist):
    t = jnp.maximum(dist, 1e-30)
    y = t * lax.rsqrt(t) * SLOPE
    return (t - y + SHIFT) * jnp.exp2(y)


OWN, CORE, HALF, BOTH = range(4)
STEPS = (0, 1, -1, 2, -2, 3, -3, 4)
PAIRS = [(OWN, 0), (CORE, 0), (OWN, 1), (CORE, 1), (OWN, 2), (CORE, 2), (CORE, 3)]
PAIRS += [(who, block) for first in (0, 4) for who in (HALF, BOTH) for block in range(first, first + 4)]
PAIRS += [(CORE, block) for block in range(4, RING)]
PAIRS += [(OWN, block) for block in range(3, RING)]
GROUP = 4
TILE, CHUNK = 256, 16
GROUPS = len(PAIRS) // GROUP
READY = {1: (3,), 3: (4, 5), 4: (6, 7)}


def block_kernel(
    own_ref, far_ref, there_ref, out_ref,
    land, other, left, right, probes, d0, d1, h0, h1, l0, l1, acc, part, back,
    land_sem, back_sem, ring_sem, part_sem, other_send, other_recv,
):
    grp, half, ring, core = coordinates()

    def place(step):
        return (ring + step + RING) % RING

    around = [member(grp, half, place(step), core) for step in STEPS]
    near = near_devices()
    barrier = enter(around[1:] + near)
    ring_to = [
        remote(far_ref, land.at[ring], ring_sem.at[at - 1], land_sem.at[ring], around[at])
        for at in range(1, RING)
    ]
    half_to = remote(own_ref.at[0:FEAT], other.at[0], other_send.at[0], other_recv.at[0], near[1])
    both_to = remote(other.at[0], other.at[1], other_send.at[1], other_recv.at[1], near[0])
    sums_to = [remote(part.at[at], back.at[at], part_sem.at[at], back_sem.at[at], near[at]) for at in range(3)]

    def block_arrived(at):
        where = place(STEPS[at])
        remote(far_ref, land.at[where], ring_sem.at[0], land_sem.at[where], around[at]).wait_recv()

    D, H, L = (d0, d1), (h0, h1), (l0, l1)

    def lift(at):
        where = place(STEPS[at])
        block = land.at[where] if at else far_ref
        right[where] = lifted(block[0:FEAT, :], False).T
        values = block[FEAT:ROWS, :]
        high = values.astype(BF16)
        probes[where] = jnp.concatenate([high, (values - high.astype(F32)).astype(BF16)], 0)

    def distances(pair, k):
        who, where = pair
        D[k][...] = dot(right[where], left[who])

    def products(pair, k):
        who, where = pair
        acc[who] += dot(probes[where], H[k][...]) + dot(probes[where], L[k][...])

    def step(pair, ahead, behind, k):
        o = 1 - k
        for c in range(0, PTS, TILE):
            for r in range(0, PTS, TILE):
                rows, cols = slice(r, r + TILE), slice(c, c + TILE)
                if ahead is not None:
                    D[o][rows, cols] = dot(right[ahead[1], rows, :], left[ahead[0], :, cols])
                for at in range(r, r + TILE, CHUNK):
                    if at == r + TILE // 2 and behind is not None:
                        weights = probes[behind[1], :, rows]
                        acc[behind[0], :, cols] += dot(weights, H[o][rows, cols]) + dot(weights, L[o][rows, cols])
                    chunk = slice(at, at + CHUNK)
                    value = matern(D[k][chunk, cols])
                    high = value.astype(BF16)
                    H[k][chunk, cols] = high
                    L[k][chunk, cols] = (value - high.astype(F32)).astype(BF16)

    def region(at, work):
        pl.when(ring < RING + at)(work)

    pairs = [(who, place(STEPS[at])) for who, at in PAIRS]
    left[OWN] = lifted(own_ref[0:FEAT, :], True)
    lift(0)
    distances(pairs[0], 0)
    left[CORE] = lifted(there_ref[...], True)
    acc[...] = jnp.zeros_like(acc)
    pl.semaphore_wait(barrier, RING - 1 + 3)
    ring_to[0].start()
    ring_to[1].start()
    half_to.start()
    for item in ring_to[2:]:
        item.start()
    region(0, lambda: step(pairs[0], pairs[1], None, 0))
    region(1, lambda: step(pairs[1], None, pairs[0], 1))
    for at in (1, 2):
        block_arrived(at)
        lift(at)
    distances(pairs[2], 0)
    region(2, lambda: step(pairs[2], pairs[3], pairs[1], 0))
    region(3, lambda: step(pairs[3], pairs[4], pairs[2], 1))

    def picked(index, values):
        result = values[0]
        for at in range(1, len(values)):
            result = jnp.where(index == at, values[at], result)
        return result

    whos = [who for who, _ in PAIRS]
    wheres = [where for _, where in pairs]

    def pair_at(n, q):
        at = [min(g * GROUP + q, len(PAIRS) - 1) for g in range(GROUPS)]
        return picked(n, [whos[i] for i in at]), picked(n, [wheres[i] for i in at])

    def send_sum(who):
        part[who - 1] = acc[who, 0:PROBES, :] + acc[who, PROBES : 2 * PROBES, :]
        sums_to[who - 1].start()

    def body(n, carry):
        for m, blocks_ready in READY.items():
            @pl.when(n == m)
            def _():
                for at in blocks_ready:
                    block_arrived(at)
                    lift(at)

        @pl.when(n == 1)
        def _():
            half_to.wait_recv()
            both_to.start()
            left[HALF] = lifted(other[0], True)

        @pl.when(n == 2)
        def _():
            both_to.wait_recv()
            left[BOTH] = lifted(other[1], True)

        @pl.when(n == 6)
        def _():
            send_sum(HALF)
            send_sum(BOTH)

        @pl.when(n == 7)
        def _():
            send_sum(CORE)

        seq = [pair_at(n, q) for q in range(-1, GROUP + 1)]
        for q in range(GROUP):
            region(n + q, functools.partial(step, seq[q + 1], seq[q + 2], seq[q], q % 2))
        return carry

    lax.fori_loop(1, GROUPS, body, 0)
    products(pairs[-1], 1)
    total = acc[OWN, 0:PROBES, :] + acc[OWN, PROBES : 2 * PROBES, :]
    for who in (HALF, BOTH, CORE):
        sums_to[who - 1].wait_recv()
        total += back[who - 1]
    out_ref[...] = total * (1.0 / SHIFT)
    for item in ring_to + [half_to, both_to] + sums_to:
        item.wait_send()


def blocks(own, far, there):
    vmem = pl.BlockSpec(memory_space=pltpu.VMEM)
    dma = pltpu.SemaphoreType.DMA
    return pl.pallas_call(
        block_kernel,
        out_shape=jax.ShapeDtypeStruct((PROBES, PTS), F32),
        in_specs=[vmem] * 3,
        out_specs=vmem,
        scratch_shapes=[
            pltpu.VMEM((RING, ROWS, PTS), F32),
            pltpu.VMEM((2, FEAT, PTS), F32),
            pltpu.VMEM((4, DEPTH, PTS), BF16),
            pltpu.VMEM((RING, PTS, DEPTH), BF16),
            pltpu.VMEM((RING, 2 * PROBES, PTS), BF16),
            pltpu.VMEM((PTS, PTS), F32),
            pltpu.VMEM((PTS, PTS), F32),
            pltpu.VMEM((PTS, PTS), BF16),
            pltpu.VMEM((PTS, PTS), BF16),
            pltpu.VMEM((PTS, PTS), BF16),
            pltpu.VMEM((PTS, PTS), BF16),
            pltpu.VMEM((4, 2 * PROBES, PTS), F32),
            pltpu.VMEM((3, PROBES, PTS), F32),
            pltpu.VMEM((3, PROBES, PTS), F32),
            dma((RING,)), dma((3,)), dma((RING - 1,)), dma((3,)), dma((2,)), dma((2,)),
        ],
        compiler_params=pltpu.CompilerParams(
            collective_id=0, has_side_effects=True, vmem_limit_bytes=32 << 20
        ),
        name="blocks",
    )(own, far, there)


def shards(points, lengthscales, probes, plan, round_index):
    shift, own = scale(round_index, plan, lengthscales, points, probes)
    far, there = lax.switch(shift[0], [functools.partial(swap, which) for which in range(1, 16)], own)
    return blocks(own, far, there)


def solution(mesh):
    in_specs = (P(None, ("grp", "mem")), P(), P(None, ("grp", "mem")), P(), P())
    out_specs = P(None, ("grp", "mem"))
    return jax.shard_map(shards, mesh=mesh, in_specs=in_specs, out_specs=out_specs, check_vma=False)
```

```python
import functools
import math

import jax
import jax.numpy as jnp
from jax import lax
from jax.experimental import pallas as pl
from jax.experimental.pallas import tpu as pltpu
from jax.sharding import PartitionSpec as P

F32, BF16 = jnp.float32, jnp.bfloat16
MESH = pl.DeviceIdType.MESH
LOG2E = math.log2(math.e)
UNIT = math.sqrt(LOG2E / 3.0)
SCALE = math.sqrt(5.0) * UNIT
SLOPE = -LOG2E / UNIT
SHIFT = 3.0 * UNIT * UNIT

FEAT, PROBES, PTS = 16, 8, 512
ROWS = FEAT + PROBES
DEPTH = 128
RING, CORES, HALVES = 8, 2, 2


def coordinates():
    grp, mem = lax.axis_index("grp"), lax.axis_index("mem")
    return grp, mem // (RING * CORES), (mem // CORES) % RING, mem % CORES


def member(grp, half, ring, core):
    return (grp, (half * RING + ring) * CORES + core)


def near_devices():
    grp, half, ring, core = coordinates()
    return [
        member(grp, half, ring, 1 - core),
        member(grp, 1 - half, ring, core),
        member(grp, 1 - half, ring, 1 - core),
    ]


def remote(src, dst, send_sem, recv_sem, device):
    return pltpu.make_async_remote_copy(
        src_ref=src, dst_ref=dst, send_sem=send_sem, recv_sem=recv_sem,
        device_id=device, device_id_type=MESH,
    )


def enter(devices):
    barrier = pltpu.get_barrier_semaphore()
    for device in devices:
        pl.semaphore_signal(barrier, inc=1, device_id=device, device_id_type=MESH)
    return barrier


def scale_kernel(round_ref, plan_ref, ls_ref, pts_ref, prb_ref, shift_ref, own_ref):
    shift_ref[0] = plan_ref[round_ref[0], 0] - 1
    row = lax.broadcasted_iota(jnp.int32, (FEAT, PTS), 0)
    scales = jnp.full((FEAT, PTS), ls_ref[0], F32)
    for feature in range(1, FEAT):
        scales = jnp.where(row == feature, ls_ref[feature], scales)
    own_ref[0:FEAT, :] = pts_ref[...] / scales * SCALE
    own_ref[FEAT:ROWS, :] = prb_ref[...]


def scale(round_index, plan, ls, points, probes):
    vmem, smem = pl.BlockSpec(memory_space=pltpu.VMEM), pl.BlockSpec(memory_space=pltpu.SMEM)
    return pl.pallas_call(
        scale_kernel,
        out_shape=[jax.ShapeDtypeStruct((1,), jnp.int32), jax.ShapeDtypeStruct((ROWS, PTS), F32)],
        in_specs=[smem, smem, smem, vmem, vmem],
        out_specs=[smem, vmem],
        name="scale",
    )(round_index, plan, ls, points, probes)


def swap_kernel(shift, own_ref, far_ref, there_ref, send_sem, recv_sem):
    grp, half, ring, core = coordinates()
    partner = grp
    for bit in range(4):
        if shift >> bit & 1:
            partner = partner + (1 - 2 * ((grp // (1 << bit)) % 2)) * (1 << bit)
    devices = [member(partner, half, ring, core), member(grp, half, ring, 1 - core)]
    barrier = enter(devices)
    pl.semaphore_wait(barrier, len(devices))
    copies = [
        remote(own_ref, far_ref, send_sem.at[0], recv_sem.at[0], devices[0]),
        remote(own_ref.at[0:FEAT], there_ref, send_sem.at[1], recv_sem.at[1], devices[1]),
    ]
    for copy in copies:
        copy.start()
    for copy in copies:
        copy.wait()


def swap(shift, own):
    vmem = pl.BlockSpec(memory_space=pltpu.VMEM)
    return pl.pallas_call(
        functools.partial(swap_kernel, shift),
        out_shape=[jax.ShapeDtypeStruct((ROWS, PTS), F32), jax.ShapeDtypeStruct((FEAT, PTS), F32)],
        in_specs=[vmem],
        out_specs=[vmem] * 2,
        scratch_shapes=[pltpu.SemaphoreType.DMA((2,)), pltpu.SemaphoreType.DMA((2,))],
        compiler_params=pltpu.CompilerParams(collective_id=shift, has_side_effects=True),
        name="swap",
    )(own)


def pieces(x):
    first = x.astype(BF16)
    rest = x - first.astype(F32)
    second = rest.astype(BF16)
    third = (rest - second.astype(F32)).astype(BF16)
    return first, second, third


def lifted(x, left):
    norm = jnp.sum(x * x, axis=0, keepdims=True)
    if left:
        x = x * -2.0
    a, b, c = pieces(x)
    row = lax.broadcasted_iota(jnp.int32, (FEAT, PTS), 0)
    first = 0 if left else 3
    ones = jnp.logical_and(row >= 3 - first, row < 6 - first)
    tail = jnp.where(ones, 1.0, 0.0)
    for index, part in enumerate(pieces(norm)):
        tail = jnp.where(row == first + index, jnp.broadcast_to(part.astype(F32), tail.shape), tail)
    tail = tail.astype(BF16)
    rows = [a, a, b, a, b, c] if left else [a, b, a, c, b, a]
    return jnp.concatenate(rows + [tail, jnp.zeros_like(tail)], 0)


def dot(a, b):
    return lax.dot_general(a, b, (((1,), (0,)), ((), ())), preferred_element_type=F32)


def matern(dist):
    t = jnp.maximum(dist, 1e-30)
    y = t * lax.rsqrt(t) * SLOPE
    return (t - y + SHIFT) * jnp.exp2(y)


OWN, CORE, HALF, BOTH = range(4)
STEPS = (0, 1, -1, 2, -2, 3, -3, 4)
PAIRS = [(OWN, 0), (CORE, 0), (OWN, 1), (CORE, 1), (OWN, 2), (CORE, 2)]
PAIRS += [(who, block) for who in (HALF, BOTH) for block in range(4)]
PAIRS += [(who, block) for first in (4, 6) for who in (HALF, BOTH) for block in range(first, first + 2)]
PAIRS += [(CORE, block) for block in range(3, RING)]
PAIRS += [(OWN, block) for block in range(3, RING)]
GROUP = 4
TILE, CHUNK = 256, 16
GROUPS = len(PAIRS) // GROUP
READY = {2: (3,), 3: (4, 5), 4: (6, 7)}


def block_kernel(
    own_ref, far_ref, there_ref, out_ref,
    land, other, left, right, probes, d0, d1, h0, h1, l0, l1, acc, part, back,
    land_sem, back_sem, ring_sem, part_sem, other_send, other_recv,
):
    grp, half, ring, core = coordinates()

    def place(step):
        return (ring + step + RING) % RING

    around = [member(grp, half, place(step), core) for step in STEPS]
    near = near_devices()
    barrier = enter(around[1:] + near)
    ring_to = [
        remote(far_ref, land.at[ring], ring_sem.at[at - 1], land_sem.at[ring], around[at])
        for at in range(1, RING)
    ]
    half_to = remote(own_ref.at[0:FEAT], other.at[0], other_send.at[0], other_recv.at[0], near[1])
    both_to = remote(other.at[0], other.at[1], other_send.at[1], other_recv.at[1], near[0])
    sums_to = [remote(part.at[at], back.at[at], part_sem.at[at], back_sem.at[at], near[at]) for at in range(3)]

    def block_arrived(at):
        where = place(STEPS[at])
        remote(far_ref, land.at[where], ring_sem.at[0], land_sem.at[where], around[at]).wait_recv()

    D, H, L = (d0, d1), (h0, h1), (l0, l1)

    def lift(at):
        where = place(STEPS[at])
        block = land.at[where] if at else far_ref
        right[where] = lifted(block[0:FEAT, :], False).T
        values = block[FEAT:ROWS, :]
        high = values.astype(BF16)
        probes[where] = jnp.concatenate([high, (values - high.astype(F32)).astype(BF16)], 0)

    def distances(pair, k):
        who, where = pair
        D[k][...] = dot(right[where], left[who])

    def products(pair, k):
        who, where = pair
        acc[who] += dot(probes[where], H[k][...]) + dot(probes[where], L[k][...])

    def step(pair, ahead, behind, k):
        o = 1 - k
        for c in range(0, PTS, TILE):
            for r in range(0, PTS, TILE):
                rows, cols = slice(r, r + TILE), slice(c, c + TILE)
                if ahead is not None:
                    D[o][rows, cols] = dot(right[ahead[1], rows, :], left[ahead[0], :, cols])
                for at in range(r, r + TILE, CHUNK):
                    if at == r + TILE // 2 and behind is not None:
                        weights = probes[behind[1], :, rows]
                        acc[behind[0], :, cols] += dot(weights, H[o][rows, cols]) + dot(weights, L[o][rows, cols])
                    chunk = slice(at, at + CHUNK)
                    value = matern(D[k][chunk, cols])
                    high = value.astype(BF16)
                    H[k][chunk, cols] = high
                    L[k][chunk, cols] = (value - high.astype(F32)).astype(BF16)

    def region(at, work):
        pl.when(ring < RING + at)(work)

    pairs = [(who, place(STEPS[at])) for who, at in PAIRS]
    left[OWN] = lifted(own_ref[0:FEAT, :], True)
    lift(0)
    distances(pairs[0], 0)
    left[CORE] = lifted(there_ref[...], True)
    acc[...] = jnp.zeros_like(acc)
    pl.semaphore_wait(barrier, RING - 1 + 3)
    ring_to[0].start()
    ring_to[1].start()
    half_to.start()
    for item in ring_to[2:]:
        item.start()
    region(0, lambda: step(pairs[0], pairs[1], None, 0))
    region(1, lambda: step(pairs[1], None, pairs[0], 1))
    for at in (1, 2):
        block_arrived(at)
        lift(at)
    distances(pairs[2], 0)
    region(2, lambda: step(pairs[2], pairs[3], pairs[1], 0))
    region(3, lambda: step(pairs[3], pairs[4], pairs[2], 1))

    def picked(index, values):
        result = values[0]
        for at in range(1, len(values)):
            result = jnp.where(index == at, values[at], result)
        return result

    whos = [who for who, _ in PAIRS]
    wheres = [where for _, where in pairs]

    def pair_at(n, q):
        at = [min(g * GROUP + q, len(PAIRS) - 1) for g in range(GROUPS)]
        return picked(n, [whos[i] for i in at]), picked(n, [wheres[i] for i in at])

    def send_sum(who):
        part[who - 1] = acc[who, 0:PROBES, :] + acc[who, PROBES : 2 * PROBES, :]
        sums_to[who - 1].start()

    def body(n, carry):
        for m, blocks_ready in READY.items():
            @pl.when(n == m)
            def _():
                for at in blocks_ready:
                    block_arrived(at)
                    lift(at)

        @pl.when(n == 1)
        def _():
            half_to.wait_recv()
            both_to.start()
            left[HALF] = lifted(other[0], True)

        @pl.when(n == 2)
        def _():
            both_to.wait_recv()
            left[BOTH] = lifted(other[1], True)

        @pl.when(n == 6)
        def _():
            send_sum(HALF)
            send_sum(BOTH)

        @pl.when(n == 7)
        def _():
            send_sum(CORE)

        seq = [pair_at(n, q) for q in range(-1, GROUP + 1)]
        for q in range(GROUP):
            region(n + q, functools.partial(step, seq[q + 1], seq[q + 2], seq[q], q % 2))
        return carry

    lax.fori_loop(1, GROUPS, body, 0)
    products(pairs[-1], 1)
    total = acc[OWN, 0:PROBES, :] + acc[OWN, PROBES : 2 * PROBES, :]
    for who in (HALF, BOTH, CORE):
        sums_to[who - 1].wait_recv()
        total += back[who - 1]
    out_ref[...] = total * (1.0 / SHIFT)
    for item in ring_to + [half_to, both_to] + sums_to:
        item.wait_send()


def blocks(own, far, there):
    vmem = pl.BlockSpec(memory_space=pltpu.VMEM)
    dma = pltpu.SemaphoreType.DMA
    return pl.pallas_call(
        block_kernel,
        out_shape=jax.ShapeDtypeStruct((PROBES, PTS), F32),
        in_specs=[vmem] * 3,
        out_specs=vmem,
        scratch_shapes=[
            pltpu.VMEM((RING, ROWS, PTS), F32),
            pltpu.VMEM((2, FEAT, PTS), F32),
            pltpu.VMEM((4, DEPTH, PTS), BF16),
            pltpu.VMEM((RING, PTS, DEPTH), BF16),
            pltpu.VMEM((RING, 2 * PROBES, PTS), BF16),
            pltpu.VMEM((PTS, PTS), F32),
            pltpu.VMEM((PTS, PTS), F32),
            pltpu.VMEM((PTS, PTS), BF16),
            pltpu.VMEM((PTS, PTS), BF16),
            pltpu.VMEM((PTS, PTS), BF16),
            pltpu.VMEM((PTS, PTS), BF16),
            pltpu.VMEM((4, 2 * PROBES, PTS), F32),
            pltpu.VMEM((3, PROBES, PTS), F32),
            pltpu.VMEM((3, PROBES, PTS), F32),
            dma((RING,)), dma((3,)), dma((RING - 1,)), dma((3,)), dma((2,)), dma((2,)),
        ],
        compiler_params=pltpu.CompilerParams(
            collective_id=0, has_side_effects=True, vmem_limit_bytes=32 << 20
        ),
        name="blocks",
    )(own, far, there)


def shards(points, lengthscales, probes, plan, round_index):
    shift, own = scale(round_index, plan, lengthscales, points, probes)
    far, there = lax.switch(shift[0], [functools.partial(swap, which) for which in range(1, 16)], own)
    return blocks(own, far, there)


def solution(mesh):
    in_specs = (P(None, ("grp", "mem")), P(), P(None, ("grp", "mem")), P(), P())
    out_specs = P(None, ("grp", "mem"))
    return jax.shard_map(shards, mesh=mesh, in_specs=in_specs, out_specs=out_specs, check_vma=False)
```
